512 devices in a mesh: dp: 16 (over y, core), ctx: 32 (over x, z).
Axes of the slice: x: 4, y: 8, z: 8, core: 2. Of those that a mesh axis runs over, the one named last changes fastest.
Arguments:
- query_proj: bfloat16 [4096, 8192], P('ctx', 'dp'), may hold values from -6 to 6
- key_proj: bfloat16 [4096, 8192], P('ctx', 'dp'), may hold values from -6 to 6
- value_proj: bfloat16 [4096, 8192], P('ctx', 'dp'), may hold values from -6 to 6
- short_taps: bfloat16 [3, 7, 8192], P(None, None, 'dp'), may hold values from -2 to 2
- medium_taps: bfloat16 [512, 128], P('dp'), may hold values from -0.5 to 0.5
- out_grad: bfloat16 [4096, 8192], P('ctx', 'dp'), may hold values from -0.09375 to 0.09375
Outputs:
- short_grad: float32 [3, 7, 8192], P(None, None, 'dp')
- medium_grad: float32 [512, 128], P('dp')
The draws below stay inside these ranges and needn't reach their ends.
All inputs are finite; a program needn't handle non-finite values.
Results may differ from the reference program's by a relative error of at most 0.0003.
Values may be sent and summed in bfloat16 or wider, within the bound.
A program may use at most 64 MiB of HBM per device.

```python
import jax
import jax.numpy as jnp
from jax import lax

D = 8192
GS = 16
FT = 128
KS = 7
G = 512
LENGTH = 4096


def level_of(own_key, shape, pieces, smallest, largest):
    loudness, own = 1.0, jax.random.fold_in(own_key, 6)
    for dim, parts in pieces:
        heights = jnp.exp(jax.random.uniform(jax.random.fold_in(own, dim), (parts,), jnp.float32, smallest / len(pieces), largest / len(pieces)))
        loudness = loudness * jnp.repeat(heights, shape[dim] // parts).reshape([-1 if axis == dim else 1 for axis in range(len(shape))])
    return loudness


def normal_values(key, dims, spread, reach, split=(), held_as=jnp.bfloat16):
    factor_of = level_of(key, dims, split, -0.22, 0.18) if split else 1.0
    array = jax.random.normal(key, dims, jnp.float32) * spread * factor_of
    return jnp.minimum(jnp.maximum(array, -reach), reach).astype(held_as)


def setup_inputs(seed: int = 0) -> dict:
    streams_of = jax.random.split(jax.random.key(seed), 7)
    return {
        "query_proj": normal_values(streams_of[0], (LENGTH, D), 1.0, 6.0, ((0, 32), (1, 16))),
        "key_proj": normal_values(streams_of[1], (LENGTH, D), 1.0, 6.0, ((0, 32), (1, 16))),
        "value_proj": normal_values(streams_of[2], (LENGTH, D), 1.0, 6.0, ((0, 32), (1, 16))),
        "short_taps": normal_values(streams_of[3], (3, KS, D), KS ** -0.5, 2.0, ((2, 16),)),
        "medium_taps": normal_values(streams_of[4], (G, FT), FT ** -0.5, 0.5, ((0, 16),)),
        "out_grad": normal_values(streams_of[5], (LENGTH, D), LENGTH ** -0.5, 0.09375, ((0, 32), (1, 16))),
    }


def short_conv(stream, conv_weights):
    summed = jnp.zeros_like(stream)
    for offset in range(KS):
        moved = jnp.pad(stream, ((offset, 0), (0, 0)))[:stream.shape[0]]
        summed = summed + conv_weights[offset] * moved
    return summed

def medium_conv(mixed, filter_weights):
    per_channel = jnp.repeat(filter_weights, GS, axis=0).T
    length_rows = mixed.shape[0]
    padded_len = 2 * length_rows
    spectrum = jnp.fft.rfft(mixed, n=padded_len, axis=0) * jnp.fft.rfft(per_channel, n=padded_len, axis=0)
    return jnp.fft.irfft(spectrum, n=padded_len, axis=0)[:length_rows]

def block_forward(query_rows, key_rows, value_rows, conv_weights, filter_weights):
    query_feat = short_conv(query_rows, conv_weights[0])
    key_feat = short_conv(key_rows, conv_weights[1])
    value_feat = short_conv(value_rows, conv_weights[2])
    return query_feat * medium_conv(key_feat * value_feat, filter_weights)

def reference(query_proj, key_proj, value_proj, short_taps, medium_taps, out_grad):
    block_width = GS * min(32, G)
    block_count = D // block_width

    def split_channels(stream):
        return stream.reshape(LENGTH, block_count, block_width).transpose(1, 0, 2)
    conv_blocks = short_taps.astype(jnp.float32).reshape(3, KS, block_count, block_width).transpose(2, 0, 1, 3)
    filter_blocks = medium_taps.astype(jnp.float32).reshape(block_count, G // block_count, FT)

    def one_block(items):
        query_rows, key_rows, value_rows, grad_rows, conv_weights, filter_weights = items

        def forward(conv_part, filter_part):
            return block_forward(query_rows.astype(jnp.float32), key_rows.astype(jnp.float32), value_rows.astype(jnp.float32), conv_part, filter_part)
        _, pullback = jax.vjp(forward, conv_weights, filter_weights)
        conv_grad, filter_grad = pullback(grad_rows.astype(jnp.float32))
        return (conv_grad, filter_grad)
    conv_total, filter_total = lax.map(one_block, (split_channels(query_proj), split_channels(key_proj), split_channels(value_proj), split_channels(out_grad), conv_blocks, filter_blocks))
    return (conv_total.transpose(1, 2, 0, 3).reshape(3, KS, D), filter_total.reshape(G, FT))
```

```python
import jax
import jax.numpy as jnp
from jax import lax
from jax.experimental import pallas as pl
from jax.experimental.pallas import tpu as pltpu
from jax.sharding import PartitionSpec as P

MESH = pl.DeviceIdType.MESH
f32, bf16 = jnp.float32, jnp.bfloat16
X, Z = 4, 8
N = X * Z
T = 128
L = 128
TILES = 4
GROUPS = 8
RIM = 16
KS = 7


def halves(x):
    hi = x.astype(bf16)
    lo = (x - hi.astype(f32)).astype(bf16)
    return jnp.concatenate([hi, lo], axis=-1)


def kernel(
    q_ref, k_ref, v_ref, w_ref, h_ref, og_ref, s_ref, m_ref,
    toep, halo_kv, halo_qg, rim, qext, kext, vext, wide, lhs, res,
    acc, ra, rb, gat,
    halo_send, halo_recv, rim_send, rim_recv, s1, r1, s2, r2, s3, r3,
):
    me = lax.axis_index("ctx")
    x, z = me // Z, lax.rem(me, Z)
    nxt = {"ctx": lax.rem(me + 1, N)}
    nxt2 = {"ctx": lax.rem(me + 2, N)}
    prv = {"ctx": lax.rem(me + N - 1, N)}
    prv2 = {"ctx": lax.rem(me + N - 2, N)}
    zs = [lax.rem(z + d, Z) for d in (4, 3, 5, 2, 6, 1, 7)]
    xs = [lax.rem(x + d, X) for d in (2, 1, 3)]

    barrier = pltpu.get_barrier_semaphore()
    partners = [prv, prv2, nxt] + [{"ctx": x * Z + p} for p in zs] + [{"ctx": p * Z + z} for p in xs]
    for p in partners:
        pl.semaphore_signal(barrier, 1, device_id=p, device_id_type=MESH)

    row = lax.broadcasted_iota(jnp.int32, (T, L), 0)
    col = lax.broadcasted_iota(jnp.int32, (T, L), 1)
    flip = jnp.where(lax.rem(row + col, L) == 0, 1.0, 0.0).astype(bf16)
    taps = h_ref[...].astype(f32)
    flipped = jnp.dot(h_ref[...], flip, preferred_element_type=f32)
    for g in range(TILES * GROUPS):
        for way, src in ((0, flipped), (1, taps)):
            ring = pltpu.roll(
                jnp.broadcast_to(src[g : g + 1], (T, L)), 0, 1, stride=1, stride_axis=0
            )
            near = (col <= row) if way == 0 else (row <= col)
            toep[way, g, :, :L] = jnp.where(near, ring, 0.0).astype(bf16)
            toep[way, g, :, L:] = jnp.where(near, 0.0, ring).astype(bf16)

    pl.semaphore_wait(barrier, len(partners))

    last = pl.ds(T - RIM, RIM)
    half = TILES // 2 * L
    copies = [
        (q_ref.at[last], rim.at[:, pl.ds(0, 512)], nxt),
        (k_ref.at[last, pl.ds(half, half)], rim.at[:, pl.ds(512, half)], nxt),
        (v_ref.at[last, pl.ds(half, half)], rim.at[:, pl.ds(768, half)], nxt),
        (k_ref.at[last, pl.ds(0, half)], rim.at[:, pl.ds(1024, half)], nxt2),
        (v_ref.at[last, pl.ds(0, half)], rim.at[:, pl.ds(1280, half)], nxt2),
    ]
    for a, b, p in copies:
        pltpu.make_async_remote_copy(a, b, rim_send, rim_recv, p, MESH).start()
    halos = [
        (k_ref.at[:, pl.ds(0, half)], halo_kv.at[0], nxt),
        (v_ref.at[:, pl.ds(0, half)], halo_kv.at[1], nxt),
        (q_ref.at[:, pl.ds(half, half)], halo_qg.at[0], prv),
        (og_ref.at[:, pl.ds(half, half)], halo_qg.at[1], prv),
    ]
    moving = []
    for n, (a, b, p) in enumerate(halos):
        c = pltpu.make_async_remote_copy(a, b, halo_send.at[n], halo_recv.at[n], p, MESH)
        c.start()
        moving.append(c)

    for t in range(TILES):
        lanes = slice(t * L, (t + 1) * L)
        qext[t, 8 : 8 + T] = q_ref[:, lanes].astype(f32)
        kext[t, 8 + T :] = k_ref[:, lanes].astype(f32)
        vext[t, 8 + T :] = v_ref[:, lanes].astype(f32)

    pltpu.make_async_copy(rim, rim, rim_recv).wait()
    for c in moving:
        c.wait()
    first = me == 0
    final = me == N - 1

    def unless(cond, v):
        return jnp.where(cond, 0.0, v.astype(f32))

    for t in range(TILES):
        lanes = slice(t * L, (t + 1) * L)
        qext[t, 0:8] = unless(first, rim[8:16, lanes])
        if t < TILES // 2:
            kext[t, 0:8] = unless(me <= 1, rim[8:16, 1024 + t * L : 1024 + (t + 1) * L])
            vext[t, 0:8] = unless(me <= 1, rim[8:16, 1280 + t * L : 1280 + (t + 1) * L])
            kext[t, 8 : 8 + T] = unless(first, halo_kv[0, :, lanes])
            vext[t, 8 : 8 + T] = unless(first, halo_kv[1, :, lanes])
        else:
            other = slice((t - 2) * L, (t - 1) * L)
            kext[t, T : T + 8] = unless(first, rim[8:16, 512 + (t - 2) * L : 512 + (t - 1) * L])
            vext[t, T : T + 8] = unless(first, rim[8:16, 768 + (t - 2) * L : 768 + (t - 1) * L])
            qext[t, 8 + T :] = unless(final, halo_qg[0, :, other])

    def featurize(stream, ext, t, start, rows):
        w = w_ref[stream, :, t * L : (t + 1) * L].astype(f32)
        total = w[0:1] * ext[t, pl.ds(start, rows)]
        for j in range(1, KS):
            total = total + w[j : j + 1] * ext[t, pl.ds(start - j, rows)]
        return total

    def tap_grad(kind, t, ext, parts):
        rows = []
        for j in range(KS):
            total = jnp.zeros((8, L), f32)
            for start, g in parts:
                total = total + jnp.sum((g * ext[t, pl.ds(start - j, T)]).reshape(T // 8, 8, L), axis=0)
            rows.append(jnp.sum(total, axis=0, keepdims=True))
        acc[t, kind] = jnp.concatenate(rows + [jnp.zeros((1, L), f32)], axis=0)

    own_group = col // 16

    def pick(values):
        out = values(0)
        for g in range(1, GROUPS):
            out = jnp.where(own_group == g, values(g), out)
        return out

    def conv(way, t, piece, rhs):
        filt = toep[way, t * GROUPS : (t + 1) * GROUPS]
        if piece is not None:
            filt = filt[:, :, piece * L : (piece + 1) * L]
        k = filt.shape[-1]
        res[0 : GROUPS * T] = jnp.dot(filt.reshape(GROUPS * T, k), rhs, preferred_element_type=f32)
        return pick(lambda g: res[g * T : (g + 1) * T, :L] + res[g * T : (g + 1) * T, L:])

    def lag_sums(t, square):
        for g in range(GROUPS):
            own = square(g)
            total = own[0:8]
            for i in range(1, T // 8):
                total = total + pltpu.roll(own[8 * i : 8 * i + 8], L - 8 * i, 1)
            wide[8 * g : 8 * g + 8] = total
        total = wide[pl.ds(0, 8, stride=8)]
        for r in range(1, 8):
            total = total + pltpu.roll(wide[pl.ds(r, 8, stride=8)], L - r, 1)
        acc[t, 3] = total

    nt = (((1,), (1,)), ((), ()))
    for t in range(TILES):
        lanes = slice(t * L, (t + 1) * L)
        og = og_ref[:, lanes].astype(f32)
        q_own = featurize(0, qext, t, 8, T)
        k_own = featurize(1, kext, t, 8 + T, T)
        v_own = featurize(2, vext, t, 8 + T, T)
        mixed = k_own * v_own
        grad = og * q_own
        m2, g2 = halves(mixed), halves(grad)
        mask = [jnp.where((lax.broadcasted_iota(jnp.int32, (T, 2 * L), 1) % L) // 16 == g, 1.0, 0.0).astype(bf16) for g in range(GROUPS)]
        if t < TILES // 2:
            k_prev = featurize(1, kext, t, 8, T)
            v_prev = featurize(2, vext, t, 8, T)
            mp2 = halves(k_prev * v_prev)
            both = jnp.concatenate([m2, mp2], axis=0)
            out = conv(0, t, None, both)
            tap_grad(0, t, qext, [(8, og * out)])
            back = conv(1, t, 0, g2)
            back_prev = conv(1, t, 1, g2)
            tap_grad(1, t, kext, [(8 + T, back * v_own), (8, back_prev * v_prev)])
            tap_grad(2, t, vext, [(8 + T, back * k_own), (8, back_prev * k_prev)])
            ghi, glo = g2[:, :L], g2[:, L:]
            rhs = jnp.concatenate([jnp.concatenate([ghi, ghi], 1), jnp.concatenate([glo, glo], 1)], 0)
            for g in range(GROUPS):
                lhs[g * 2 * T : g * 2 * T + T] = m2 * mask[g]
                lhs[g * 2 * T + T : (g + 1) * 2 * T] = mp2 * mask[g]
            res[...] = lax.dot_general(lhs[...], rhs, nt, preferred_element_type=f32)

            def square(g):
                a = res[g * 2 * T : g * 2 * T + T]
                b = res[g * 2 * T + T : (g + 1) * 2 * T]
                return jnp.where(row <= col, a[:, :L] + a[:, L:], b[:, :L] + b[:, L:])
        else:
            other = slice((t - 2) * L, (t - 1) * L)
            og_next = unless(final, halo_qg[1, :, other])
            q_next = featurize(0, qext, t, 8 + T, T)
            gn2 = halves(og_next * q_next)
            both = jnp.concatenate([g2, gn2], axis=0)
            out = conv(0, t, 0, m2)
            out_next = conv(0, t, 1, m2)
            tap_grad(0, t, qext, [(8, og * out), (8 + T, og_next * out_next)])
            back = conv(1, t, None, both)
            tap_grad(1, t, kext, [(8 + T, back * v_own)])
            tap_grad(2, t, vext, [(8 + T, back * k_own)])
            hi, lo = both[:, :L], both[:, L:]
            for g in range(GROUPS):
                lhs[g * T : (g + 1) * T] = m2 * mask[g]
            left = lhs[0 : GROUPS * T]
            res[0 : GROUPS * T] = lax.dot_general(
                left, jnp.concatenate([hi, hi], 1), nt, preferred_element_type=f32
            ) + lax.dot_general(left, jnp.concatenate([lo, lo], 1), nt, preferred_element_type=f32)

            def square(g):
                a = res[g * T : (g + 1) * T]
                return jnp.where(row <= col, a[:, :L], a[:, L:])
        lag_sums(t, square)

    for p in xs:
        pltpu.make_async_remote_copy(acc.at[p], ra.at[x], s1, r1, {"ctx": p * Z + z}, MESH).start()
    ra[x] = acc[x]
    three = ra.at[pl.ds(0, X - 1)]
    seven = rb.at[pl.ds(0, Z - 1)]
    pltpu.make_async_copy(three, three, r1).wait()
    total = ra[0]
    for i in range(1, X):
        total = total + ra[i]
    rb[z] = total
    for p in zs:
        pltpu.make_async_remote_copy(rb.at[z], rb.at[z], s2, r2, {"ctx": x * Z + p}, MESH).start()
    pltpu.make_async_copy(seven, seven, r2).wait()
    total = rb[0]
    for i in range(1, Z):
        total = total + rb[i]
    gat[x] = total
    for p in xs:
        pltpu.make_async_remote_copy(gat.at[x], gat.at[x], s3, r3, {"ctx": p * Z + z}, MESH).start()
    gathered = gat.at[pl.ds(0, X - 1)]
    pltpu.make_async_copy(gathered, gathered, r3).wait()
    for t in range(TILES):
        for kind in range(3):
            s_ref[kind, :, t * L : (t + 1) * L] = gat[t, kind, :KS]
        m_ref[t * GROUPS : (t + 1) * GROUPS] = gat[t, 3]
    pltpu.make_async_copy(rim, rim, rim_send).wait()
    pltpu.make_async_copy(three, three, s1).wait()
    pltpu.make_async_copy(seven, seven, s2).wait()
    pltpu.make_async_copy(gathered, gathered, s3).wait()


def local(q, k, v, w, h, og):
    V = pltpu.VMEM
    dma = pltpu.SemaphoreType.DMA
    return pl.pallas_call(
        kernel,
        out_shape=(jax.ShapeDtypeStruct((3, KS, 512), f32), jax.ShapeDtypeStruct((32, 128), f32)),
        in_specs=[pl.BlockSpec(memory_space=V)] * 6,
        out_specs=[pl.BlockSpec(memory_space=V)] * 2,
        scratch_shapes=[
            V((2, 32, T, 2 * L), bf16),
            V((2, T, 256), bf16),
            V((2, T, 256), bf16),
            V((RIM, 1536), bf16),
            V((TILES, 8 + 2 * T, L), f32),
            V((TILES, 8 + 2 * T, L), f32),
            V((TILES, 8 + 2 * T, L), f32),
            V((8 * GROUPS, L), f32),
            V((GROUPS * 2 * T, 2 * L), bf16),
            V((GROUPS * 2 * T, 2 * L), f32),
            V((TILES, 4, 8, L), f32),
            V((X, 4, 8, L), f32),
            V((Z, 4, 8, L), f32),
            V((TILES, 4, 8, L), f32),
            dma((4,)), dma((4,)), dma, dma, dma, dma, dma, dma, dma, dma,
        ],
        compiler_params=pltpu.CompilerParams(
            collective_id=0, has_side_effects=True, vmem_limit_bytes=48 << 20
        ),
        name="block",
    )(q, k, v, w, h, og)


def solution(mesh):
    return jax.shard_map(
        local,
        mesh=mesh,
        in_specs=(
            P("ctx", "dp"),
            P("ctx", "dp"),
            P("ctx", "dp"),
            P(None, None, "dp"),
            P("dp", None),
            P("ctx", "dp"),
        ),
        out_specs=(P(None, None, "dp"), P("dp", None)),
        check_vma=False,
    )
```

```python
import jax
import jax.numpy as jnp
from jax import lax
from jax.experimental import pallas as pl
from jax.experimental.pallas import tpu as pltpu
from jax.sharding import PartitionSpec as P

MESH = pl.DeviceIdType.MESH
f32, bf16 = jnp.float32, jnp.bfloat16
X, Z = 4, 8
N = X * Z
T = 128
L = 128
TILES = 4
GROUPS = 8
RIM = 16
KS = 7


def halves(x):
    hi = x.astype(bf16)
    lo = (x - hi.astype(f32)).astype(bf16)
    return jnp.concatenate([hi, lo], axis=-1)


def kernel(
    q_hbm, k_hbm, v_hbm, w_ref, h_ref, og_hbm, gat,
    q_ref, k_ref, v_ref, og_ref, toep, halo, rim, qext, kext, vext, wide, lhs, res,
    feats, m2s, g2s, kept, acc, ra, rb,
    loaded, halo_send, halo_recv, rim_send, rim_recv, s1, r1, s2, r2, s3, r3,
):
    me = lax.axis_index("ctx")
    x, z = me // Z, lax.rem(me, Z)
    nxt = {"ctx": lax.rem(me + 1, N)}
    nxt2 = {"ctx": lax.rem(me + 2, N)}
    prv = {"ctx": lax.rem(me + N - 1, N)}
    prv2 = {"ctx": lax.rem(me + N - 2, N)}
    zs = [lax.rem(z + d, Z) for d in (4, 3, 5, 2, 6, 1, 7)]
    xs = [lax.rem(x + d, X) for d in (2, 1, 3)]
    first = me == 0
    final = me == N - 1
    F = TILES // 2

    barrier = pltpu.get_barrier_semaphore()
    partners = [prv, prv2, nxt] + [{"ctx": x * Z + p} for p in zs] + [{"ctx": p * Z + z} for p in xs]
    for p in partners:
        pl.semaphore_signal(barrier, 1, device_id=p, device_id_type=MESH)
    loads = [
        pltpu.make_async_copy(src, dst, loaded.at[n])
        for n, (src, dst) in enumerate(
            ((q_hbm, q_ref), (k_hbm, k_ref), (v_hbm, v_ref), (og_hbm, og_ref))
        )
    ]
    for c in loads:
        c.start()
    pl.semaphore_wait(barrier, len(partners))

    last = pl.ds(T - RIM, RIM)
    half = F * L
    for a, b, p in [
        (q_hbm.at[last], rim.at[:, pl.ds(0, 512)], nxt),
        (k_hbm.at[last], rim.at[:, pl.ds(512, 512)], nxt),
        (v_hbm.at[last], rim.at[:, pl.ds(1024, 512)], nxt),
        (k_hbm.at[last, pl.ds(0, half)], rim.at[:, pl.ds(1536, half)], nxt2),
        (v_hbm.at[last, pl.ds(0, half)], rim.at[:, pl.ds(1792, half)], nxt2),
    ]:
        pltpu.make_async_remote_copy(a, b, rim_send, rim_recv, p, MESH).start()
    order = [t for pair in zip(range(F), range(F, TILES)) for t in pair]
    for t in order:
        pair, p = ((k_hbm, v_hbm), nxt) if t < F else ((q_hbm, og_hbm), prv)
        for n, src in enumerate(pair):
            pltpu.make_async_remote_copy(
                src.at[:, pl.ds(t * L, L)], halo.at[t, n], halo_send.at[t], halo_recv.at[t], p, MESH
            ).start()

    row = lax.broadcasted_iota(jnp.int32, (T, L), 0)
    col = lax.broadcasted_iota(jnp.int32, (T, L), 1)
    flip = jnp.where(lax.rem(row + col, L) == 0, 1.0, 0.0).astype(bf16)
    taps = h_ref[...].astype(f32)
    flipped = jnp.dot(h_ref[...], flip, preferred_element_type=f32)
    for g in range(TILES * GROUPS):
        for way, src in ((0, flipped), (1, taps)):
            ring = pltpu.roll(
                jnp.broadcast_to(src[g : g + 1], (T, L)), 0, 1, stride=1, stride_axis=0
            )
            near = (col <= row) if way == 0 else (row <= col)
            toep[way, 0, g] = jnp.where(near, ring, 0.0).astype(bf16)
            toep[way, 1, g] = jnp.where(near, 0.0, ring).astype(bf16)

    for c in loads:
        c.wait()
    for t in range(TILES):
        lanes = slice(t * L, (t + 1) * L)
        qext[t, 8 : 8 + T] = q_ref[:, lanes].astype(f32)
        kext[t, 8 + T :] = k_ref[:, lanes].astype(f32)
        vext[t, 8 + T :] = v_ref[:, lanes].astype(f32)

    def unless(cond, v):
        return jnp.where(cond, 0.0, v.astype(f32))

    pltpu.make_async_copy(rim, rim, rim_recv).wait()
    for t in range(TILES):
        lanes = slice(t * L, (t + 1) * L)
        qext[t, 0:8] = unless(first, rim[8:16, lanes])
        kext[t, T : T + 8] = unless(first, rim[8:16, 512 + t * L : 512 + (t + 1) * L])
        vext[t, T : T + 8] = unless(first, rim[8:16, 1024 + t * L : 1024 + (t + 1) * L])
        if t < F:
            kext[t, 0:8] = unless(me <= 1, rim[8:16, 1536 + t * L : 1536 + (t + 1) * L])
            vext[t, 0:8] = unless(me <= 1, rim[8:16, 1792 + t * L : 1792 + (t + 1) * L])

    def featurize(stream, ext, t, start, rows):
        w = w_ref[stream, :, t * L : (t + 1) * L].astype(f32)
        total = w[0:1] * ext[t, pl.ds(start, rows)]
        for j in range(1, KS):
            total = total + w[j : j + 1] * ext[t, pl.ds(start - j, rows)]
        return total

    def tap_grad(kind, t, ext, parts):
        rows = []
        for j in range(KS):
            total = jnp.zeros((8, L), f32)
            for start, g in parts:
                total = total + jnp.sum((g * ext[t, pl.ds(start - j, T)]).reshape(T // 8, 8, L), axis=0)
            rows.append(jnp.sum(total, axis=0, keepdims=True))
        return jnp.concatenate(rows + [jnp.zeros((1, L), f32)], axis=0)

    lane_group = col // 16
    wide_group = jnp.concatenate([lane_group, lane_group], axis=1)
    mask = [jnp.where(wide_group == g, 1.0, 0.0).astype(bf16) for g in range(GROUPS)]
    inside, across, both = (0,), (1,), (0, 1)
    nt = (((1,), (1,)), ((), ()))
    turn = [0]

    def result():
        turn[0] = (turn[0] + 1) % res.shape[0]
        return res.at[turn[0]]

    def conv(way, lags, t, field):
        out = result()
        filt = [toep[way, n, t * GROUPS : (t + 1) * GROUPS].reshape(GROUPS * T, T) for n in lags]
        filt = jnp.concatenate(filt, axis=1)
        out[...] = jnp.dot(filt, field, preferred_element_type=f32)
        total = out[0:T, :L] + out[0:T, L:]
        for g in range(1, GROUPS):
            total = jnp.where(lane_group == g, out[g * T : (g + 1) * T, :L] + out[g * T : (g + 1) * T, L:], total)
        return total

    def lag_sums(mix, grad, far):
        hi, lo = grad[:, :L], grad[:, L:]
        rhs = jnp.concatenate([jnp.concatenate([hi, hi], 1), jnp.concatenate([lo, lo], 1)], 0)
        for g in range(GROUPS):
            lhs[g * T : (g + 1) * T] = mix * mask[g]
        out = result()
        out[...] = lax.dot_general(lhs[...], rhs, nt, preferred_element_type=f32)
        near = row <= col
        for g in range(GROUPS):
            own = out[g * T : (g + 1) * T, :L] + out[g * T : (g + 1) * T, L:]
            own = jnp.where(near, 0.0, own) if far else jnp.where(near, own, 0.0)
            total = own[0:8]
            for i in range(1, T // 8):
                total = total + pltpu.roll(own[8 * i : 8 * i + 8], L - 8 * i, 1)
            wide[8 * g : 8 * g + 8] = total
        total = wide[pl.ds(0, 8, stride=8)]
        for r in range(1, 8):
            total = total + pltpu.roll(wide[pl.ds(r, 8, stride=8)], L - r, 1)
        return total

    for t in order:
        og = og_ref[:, t * L : (t + 1) * L].astype(f32)
        q_own = featurize(0, qext, t, 8, T)
        k_own = featurize(1, kext, t, 8 + T, T)
        v_own = featurize(2, vext, t, 8 + T, T)
        m2s[t], g2s[t] = halves(k_own * v_own), halves(og * q_own)
        if t < F:
            back = conv(1, inside, t, g2s[t])
            kept[t] = conv(1, across, t, g2s[t])
            acc[t, 1] = tap_grad(1, t, kext, [(8 + T, back * v_own)])
            acc[t, 2] = tap_grad(2, t, vext, [(8 + T, back * k_own)])
        else:
            out = conv(0, inside, t, m2s[t])
            kept[t] = conv(0, across, t, m2s[t])
            feats[t - F, 0], feats[t - F, 1] = k_own, v_own
            acc[t, 0] = tap_grad(0, t, qext, [(8, og * out)])
        acc[t, 3] = lag_sums(m2s[t], g2s[t], False)

    for t in order:
        pltpu.make_async_copy(halo.at[t], halo.at[t], halo_recv.at[t]).wait()
        if t < F:
            kext[t, 8 : 8 + T] = unless(first, halo[t, 0])
            vext[t, 8 : 8 + T] = unless(first, halo[t, 1])
            og = og_ref[:, t * L : (t + 1) * L].astype(f32)
            k_prev = featurize(1, kext, t, 8, T)
            v_prev = featurize(2, vext, t, 8, T)
            mp2 = halves(k_prev * v_prev)
            out = conv(0, both, t, jnp.concatenate([m2s[t], mp2], axis=0))
            back = kept[t]
            acc[t, 0] = tap_grad(0, t, qext, [(8, og * out)])
            acc[t, 1] += tap_grad(1, t, kext, [(8, back * v_prev)])
            acc[t, 2] += tap_grad(2, t, vext, [(8, back * k_prev)])
            acc[t, 3] += lag_sums(mp2, g2s[t], True)
        else:
            qext[t, 8 + T :] = unless(final, halo[t, 0])
            og_next = unless(final, halo[t, 1])
            gn2 = halves(og_next * featurize(0, qext, t, 8 + T, T))
            back = conv(1, both, t, jnp.concatenate([g2s[t], gn2], axis=0))
            acc[t, 0] += tap_grad(0, t, qext, [(8 + T, og_next * kept[t])])
            acc[t, 1] = tap_grad(1, t, kext, [(8 + T, back * feats[t - F, 1])])
            acc[t, 2] = tap_grad(2, t, vext, [(8 + T, back * feats[t - F, 0])])
            acc[t, 3] += lag_sums(m2s[t], gn2, True)

        @pl.when(x != t)
        def _():
            pltpu.make_async_remote_copy(acc.at[t], ra.at[x], s1, r1, {"ctx": t * Z + z}, MESH).start()

    ra[x] = acc[x]
    three = ra.at[pl.ds(0, X - 1)]
    seven = rb.at[pl.ds(0, Z - 1)]
    pltpu.make_async_copy(three, three, r1).wait()
    total = ra[0]
    for i in range(1, X):
        total = total + ra[i]
    rb[z] = total
    for p in zs:
        pltpu.make_async_remote_copy(rb.at[z], rb.at[z], s2, r2, {"ctx": x * Z + p}, MESH).start()
    pltpu.make_async_copy(seven, seven, r2).wait()
    total = rb[0]
    for i in range(1, Z):
        total = total + rb[i]
    gat[x] = total
    for p in xs:
        pltpu.make_async_remote_copy(gat.at[x], gat.at[x], s3, r3, {"ctx": p * Z + z}, MESH).start()
    gathered = gat.at[pl.ds(0, X - 1)]
    pltpu.make_async_copy(gathered, gathered, r3).wait()
    for t in order:
        pltpu.make_async_copy(halo.at[t], halo.at[t], halo_send.at[t]).wait()
    pltpu.make_async_copy(rim, rim, rim_send).wait()
    pltpu.make_async_copy(three, three, s1).wait()
    pltpu.make_async_copy(seven, seven, s2).wait()
    pltpu.make_async_copy(gathered, gathered, s3).wait()


def spread(gat, s_ref, m_ref):
    for t in range(TILES):
        for kind in range(3):
            s_ref[kind, :, t * L : (t + 1) * L] = gat[t, kind, :KS]
        m_ref[t * GROUPS : (t + 1) * GROUPS] = gat[t, 3]


def local(q, k, v, w, h, og):
    V = pltpu.VMEM
    dma = pltpu.SemaphoreType.DMA
    hbm, vmem = pl.BlockSpec(memory_space=pltpu.HBM), pl.BlockSpec(memory_space=V)
    sums = pl.pallas_call(
        kernel,
        out_shape=jax.ShapeDtypeStruct((TILES, 4, 8, L), f32),
        in_specs=[hbm, hbm, hbm, vmem, vmem, hbm],
        out_specs=vmem,
        scratch_shapes=[
            V((T, 512), bf16), V((T, 512), bf16), V((T, 512), bf16), V((T, 512), bf16),
            V((2, 2, TILES * GROUPS, T, T), bf16),
            V((TILES, 2, T, L), bf16),
            V((RIM, 2048), bf16),
            V((TILES, 8 + 2 * T, L), f32),
            V((TILES, 8 + 2 * T, L), f32),
            V((TILES, 8 + 2 * T, L), f32),
            V((8 * GROUPS, L), f32),
            V((GROUPS * T, 2 * L), bf16),
            V((4, GROUPS * T, 2 * L), f32),
            V((2, 2, T, L), f32),
            V((TILES, T, 2 * L), bf16),
            V((TILES, T, 2 * L), bf16),
            V((TILES, T, L), f32),
            V((TILES, 4, 8, L), f32),
            V((X, 4, 8, L), f32),
            V((Z, 4, 8, L), f32),
            dma((4,)), dma((TILES,)), dma((TILES,)),
            dma, dma, dma, dma, dma, dma, dma, dma,
        ],
        compiler_params=pltpu.CompilerParams(
            collective_id=0, has_side_effects=True, vmem_limit_bytes=64 << 20
        ),
        name="block",
    )(q, k, v, w, h, og)
    return pl.pallas_call(
        spread,
        out_shape=(jax.ShapeDtypeStruct((3, KS, 512), f32), jax.ShapeDtypeStruct((32, 128), f32)),
        in_specs=[vmem],
        out_specs=[vmem, vmem],
        name="spread",
    )(sums)


def solution(mesh):
    return jax.shard_map(
        local,
        mesh=mesh,
        in_specs=(
            P("ctx", "dp"),
            P("ctx", "dp"),
            P("ctx", "dp"),
            P(None, None, "dp"),
            P("dp", None),
            P("ctx", "dp"),
        ),
        out_specs=(P(None, None, "dp"), P("dp", None)),
        check_vma=False,
    )
```

```python
import jax
import jax.numpy as jnp
from jax import lax
from jax.experimental import pallas as pl
from jax.experimental.pallas import tpu as pltpu
from jax.sharding import PartitionSpec as P

MESH = pl.DeviceIdType.MESH
f32, bf16 = jnp.float32, jnp.bfloat16
X, Z = 4, 8
N = X * Z
T = 128
L = 128
TILES = 4
GROUPS = 8
RIM = 16
KS = 7


def halves(x):
    hi = x.astype(bf16)
    lo = (x - hi.astype(f32)).astype(bf16)
    return jnp.concatenate([hi, lo], axis=-1)


def kernel(
    q_hbm, k_hbm, v_hbm, w_hbm, h_hbm, og_hbm, gat,
    q_ref, k_ref, v_ref, w_ref, h_ref, og_ref, toep, halo, rim, qext, kext, vext, wide, lhs, res,
    feats, m2s, g2s, kept, acc, ra, rb,
    loaded, halo_send, halo_recv, rim_send, rim_recv, s1, r1, s2, r2, s3, r3,
):
    me = lax.axis_index("ctx")
    x, z = me // Z, lax.rem(me, Z)
    nxt = {"ctx": lax.rem(me + 1, N)}
    nxt2 = {"ctx": lax.rem(me + 2, N)}
    prv = {"ctx": lax.rem(me + N - 1, N)}
    prv2 = {"ctx": lax.rem(me + N - 2, N)}
    zs = [lax.rem(z + d, Z) for d in (4, 3, 5, 2, 6, 1, 7)]
    xs = [lax.rem(x + d, X) for d in (2, 1, 3)]
    first = me == 0
    final = me == N - 1
    F = TILES // 2

    barrier = pltpu.get_barrier_semaphore()
    partners = [prv, prv2, nxt] + [{"ctx": x * Z + p} for p in zs] + [{"ctx": p * Z + z} for p in xs]
    for p in partners:
        pl.semaphore_signal(barrier, 1, device_id=p, device_id_type=MESH)
    loads = [
        pltpu.make_async_copy(src, dst, loaded.at[n])
        for n, (src, dst) in enumerate(
            ((h_hbm, h_ref), (q_hbm, q_ref), (k_hbm, k_ref), (v_hbm, v_ref), (og_hbm, og_ref), (w_hbm, w_ref))
        )
    ]
    for c in loads:
        c.start()
    pl.semaphore_wait(barrier, len(partners))

    last = pl.ds(T - RIM, RIM)
    half = F * L
    for a, b, p in [
        (q_hbm.at[last], rim.at[:, pl.ds(0, 512)], nxt),
        (k_hbm.at[last], rim.at[:, pl.ds(512, 512)], nxt),
        (v_hbm.at[last], rim.at[:, pl.ds(1024, 512)], nxt),
        (k_hbm.at[last, pl.ds(0, half)], rim.at[:, pl.ds(1536, half)], nxt2),
        (v_hbm.at[last, pl.ds(0, half)], rim.at[:, pl.ds(1792, half)], nxt2),
    ]:
        pltpu.make_async_remote_copy(a, b, rim_send, rim_recv, p, MESH).start()
    order = [t for pair in zip(range(F), range(F, TILES)) for t in pair]
    for t in order:
        pair, p = ((k_hbm, v_hbm), nxt) if t < F else ((q_hbm, og_hbm), prv)
        for n, src in enumerate(pair):
            pltpu.make_async_remote_copy(
                src.at[:, pl.ds(t * L, L)], halo.at[t, n], halo_send.at[t], halo_recv.at[t], p, MESH
            ).start()

    row = lax.broadcasted_iota(jnp.int32, (T, L), 0)
    col = lax.broadcasted_iota(jnp.int32, (T, L), 1)
    flip = jnp.where(lax.rem(row + col, L) == 0, 1.0, 0.0).astype(bf16)
    loads[0].wait()
    taps = h_ref[...].astype(f32)
    flipped = jnp.dot(h_ref[...], flip, preferred_element_type=f32)
    for g in range(TILES * GROUPS):
        for way, src in ((0, flipped), (1, taps)):
            ring = pltpu.roll(
                jnp.broadcast_to(src[g : g + 1], (T, L)), 0, 1, stride=1, stride_axis=0
            )
            near = (col <= row) if way == 0 else (row <= col)
            toep[way, 0, g] = jnp.where(near, ring, 0.0).astype(bf16)
            toep[way, 1, g] = jnp.where(near, 0.0, ring).astype(bf16)

    for c in loads[1:]:
        c.wait()
    for t in range(TILES):
        lanes = slice(t * L, (t + 1) * L)
        qext[t, 8 : 8 + T] = q_ref[:, lanes].astype(f32)
        kext[t, 8 + T :] = k_ref[:, lanes].astype(f32)
        vext[t, 8 + T :] = v_ref[:, lanes].astype(f32)

    def unless(cond, v):
        return jnp.where(cond, 0.0, v.astype(f32))

    pltpu.make_async_copy(rim, rim, rim_recv).wait()
    for t in range(TILES):
        lanes = slice(t * L, (t + 1) * L)
        qext[t, 0:8] = unless(first, rim[8:16, lanes])
        kext[t, T : T + 8] = unless(first, rim[8:16, 512 + t * L : 512 + (t + 1) * L])
        vext[t, T : T + 8] = unless(first, rim[8:16, 1024 + t * L : 1024 + (t + 1) * L])
        if t < F:
            kext[t, 0:8] = unless(me <= 1, rim[8:16, 1536 + t * L : 1536 + (t + 1) * L])
            vext[t, 0:8] = unless(me <= 1, rim[8:16, 1792 + t * L : 1792 + (t + 1) * L])

    def featurize(stream, ext, t, start, rows):
        w = w_ref[stream, :, t * L : (t + 1) * L].astype(f32)
        total = w[0:1] * ext[t, pl.ds(start, rows)]
        for j in range(1, KS):
            total = total + w[j : j + 1] * ext[t, pl.ds(start - j, rows)]
        return total

    def tap_grad(kind, t, ext, parts):
        rows = []
        for j in range(KS):
            total = jnp.zeros((8, L), f32)
            for start, g in parts:
                total = total + jnp.sum((g * ext[t, pl.ds(start - j, T)]).reshape(T // 8, 8, L), axis=0)
            rows.append(jnp.sum(total, axis=0, keepdims=True))
        return jnp.concatenate(rows + [jnp.zeros((1, L), f32)], axis=0)

    lane_group = col // 16
    wide_group = jnp.concatenate([lane_group, lane_group], axis=1)
    mask = [jnp.where(wide_group == g, 1.0, 0.0).astype(bf16) for g in range(GROUPS)]
    inside, across, both = (0,), (1,), (0, 1)
    nt = (((1,), (1,)), ((), ()))
    turn = [0]

    def result():
        turn[0] = (turn[0] + 1) % res.shape[0]
        return res.at[turn[0]]

    def conv(way, lags, t, field):
        out = result()
        filt = [toep[way, n, t * GROUPS : (t + 1) * GROUPS].reshape(GROUPS * T, T) for n in lags]
        filt = jnp.concatenate(filt, axis=1)
        out[...] = jnp.dot(filt, field, preferred_element_type=f32)
        total = out[0:T, :L] + out[0:T, L:]
        for g in range(1, GROUPS):
            total = jnp.where(lane_group == g, out[g * T : (g + 1) * T, :L] + out[g * T : (g + 1) * T, L:], total)
        return total

    def lag_sums(mix, grad, far):
        hi, lo = grad[:, :L], grad[:, L:]
        rhs = jnp.concatenate([jnp.concatenate([hi, hi], 1), jnp.concatenate([lo, lo], 1)], 0)
        for g in range(GROUPS):
            lhs[g * T : (g + 1) * T] = mix * mask[g]
        out = result()
        out[...] = lax.dot_general(lhs[...], rhs, nt, preferred_element_type=f32)
        near = row <= col
        for g in range(GROUPS):
            own = out[g * T : (g + 1) * T, :L] + out[g * T : (g + 1) * T, L:]
            own = jnp.where(near, 0.0, own) if far else jnp.where(near, own, 0.0)
            total = own[0:8]
            for i in range(1, T // 8):
                total = total + pltpu.roll(own[8 * i : 8 * i + 8], L - 8 * i, 1)
            wide[8 * g : 8 * g + 8] = total
        total = wide[pl.ds(0, 8, stride=8)]
        for r in range(1, 8):
            total = total + pltpu.roll(wide[pl.ds(r, 8, stride=8)], L - r, 1)
        return total

    for t in order:
        og = og_ref[:, t * L : (t + 1) * L].astype(f32)
        q_own = featurize(0, qext, t, 8, T)
        k_own = featurize(1, kext, t, 8 + T, T)
        v_own = featurize(2, vext, t, 8 + T, T)
        m2s[t], g2s[t] = halves(k_own * v_own), halves(og * q_own)
        if t < F:
            back = conv(1, inside, t, g2s[t])
            kept[t] = conv(1, across, t, g2s[t])
            acc[t, 1] = tap_grad(1, t, kext, [(8 + T, back * v_own)])
            acc[t, 2] = tap_grad(2, t, vext, [(8 + T, back * k_own)])
        else:
            out = conv(0, inside, t, m2s[t])
            kept[t] = conv(0, across, t, m2s[t])
            feats[t - F, 0], feats[t - F, 1] = k_own, v_own
            acc[t, 0] = tap_grad(0, t, qext, [(8, og * out)])
        acc[t, 3] = lag_sums(m2s[t], g2s[t], False)

    for t in order:
        pltpu.make_async_copy(halo.at[t], halo.at[t], halo_recv.at[t]).wait()
        if t < F:
            kext[t, 8 : 8 + T] = unless(first, halo[t, 0])
            vext[t, 8 : 8 + T] = unless(first, halo[t, 1])
            og = og_ref[:, t * L : (t + 1) * L].astype(f32)
            k_prev = featurize(1, kext, t, 8, T)
            v_prev = featurize(2, vext, t, 8, T)
            mp2 = halves(k_prev * v_prev)
            out = conv(0, both, t, jnp.concatenate([m2s[t], mp2], axis=0))
            back = kept[t]
            acc[t, 0] = tap_grad(0, t, qext, [(8, og * out)])
            acc[t, 1] += tap_grad(1, t, kext, [(8, back * v_prev)])
            acc[t, 2] += tap_grad(2, t, vext, [(8, back * k_prev)])
            acc[t, 3] += lag_sums(mp2, g2s[t], True)
        else:
            qext[t, 8 + T :] = unless(final, halo[t, 0])
            og_next = unless(final, halo[t, 1])
            gn2 = halves(og_next * featurize(0, qext, t, 8 + T, T))
            back = conv(1, both, t, jnp.concatenate([g2s[t], gn2], axis=0))
            acc[t, 0] += tap_grad(0, t, qext, [(8 + T, og_next * kept[t])])
            acc[t, 1] = tap_grad(1, t, kext, [(8 + T, back * feats[t - F, 1])])
            acc[t, 2] = tap_grad(2, t, vext, [(8 + T, back * feats[t - F, 0])])
            acc[t, 3] += lag_sums(m2s[t], gn2, True)

        @pl.when(x != t)
        def _():
            pltpu.make_async_remote_copy(acc.at[t], ra.at[x], s1, r1, {"ctx": t * Z + z}, MESH).start()

    ra[x] = acc[x]
    three = ra.at[pl.ds(0, X - 1)]
    seven = rb.at[pl.ds(0, Z - 1)]
    pltpu.make_async_copy(three, three, r1).wait()
    total = ra[0]
    for i in range(1, X):
        total = total + ra[i]
    rb[z] = total
    for p in zs:
        pltpu.make_async_remote_copy(rb.at[z], rb.at[z], s2, r2, {"ctx": x * Z + p}, MESH).start()
    pltpu.make_async_copy(seven, seven, r2).wait()
    total = rb[0]
    for i in range(1, Z):
        total = total + rb[i]
    gat[x] = total
    for p in xs:
        pltpu.make_async_remote_copy(gat.at[x], gat.at[x], s3, r3, {"ctx": p * Z + z}, MESH).start()
    gathered = gat.at[pl.ds(0, X - 1)]
    pltpu.make_async_copy(gathered, gathered, r3).wait()
    for t in order:
        pltpu.make_async_copy(halo.at[t], halo.at[t], halo_send.at[t]).wait()
    pltpu.make_async_copy(rim, rim, rim_send).wait()
    pltpu.make_async_copy(three, three, s1).wait()
    pltpu.make_async_copy(seven, seven, s2).wait()
    pltpu.make_async_copy(gathered, gathered, s3).wait()


def spread(gat, s_ref, m_ref):
    for t in range(TILES):
        for kind in range(3):
            s_ref[kind, :, t * L : (t + 1) * L] = gat[t, kind, :KS]
        m_ref[t * GROUPS : (t + 1) * GROUPS] = gat[t, 3]


def local(q, k, v, w, h, og):
    V = pltpu.VMEM
    dma = pltpu.SemaphoreType.DMA
    hbm, vmem = pl.BlockSpec(memory_space=pltpu.HBM), pl.BlockSpec(memory_space=V)
    sums = pl.pallas_call(
        kernel,
        out_shape=pltpu.VMEM((TILES, 4, 8, L), f32),
        in_specs=[hbm] * 6,
        out_specs=vmem,
        scratch_shapes=[
            V((T, 512), bf16), V((T, 512), bf16), V((T, 512), bf16), V((3, KS, 512), bf16), V((32, T), bf16), V((T, 512), bf16),
            V((2, 2, TILES * GROUPS, T, T), bf16),
            V((TILES, 2, T, L), bf16),
            V((RIM, 2048), bf16),
            V((TILES, 8 + 2 * T, L), f32),
            V((TILES, 8 + 2 * T, L), f32),
            V((TILES, 8 + 2 * T, L), f32),
            V((8 * GROUPS, L), f32),
            V((GROUPS * T, 2 * L), bf16),
            V((4, GROUPS * T, 2 * L), f32),
            V((2, 2, T, L), f32),
            V((TILES, T, 2 * L), bf16),
            V((TILES, T, 2 * L), bf16),
            V((TILES, T, L), f32),
            V((TILES, 4, 8, L), f32),
            V((X, 4, 8, L), f32),
            V((Z, 4, 8, L), f32),
            dma((6,)), dma((TILES,)), dma((TILES,)),
            dma, dma, dma, dma, dma, dma, dma, dma,
        ],
        compiler_params=pltpu.CompilerParams(
            collective_id=0, has_side_effects=True, vmem_limit_bytes=56 << 20
        ),
        name="block",
    )(q, k, v, w, h, og)
    return pl.pallas_call(
        spread,
        out_shape=(jax.ShapeDtypeStruct((3, KS, 512), f32), jax.ShapeDtypeStruct((32, 128), f32)),
        in_specs=[vmem],
        out_specs=[vmem, vmem],
        compiler_params=pltpu.CompilerParams(vmem_limit_bytes=1 << 20),
        name="spread",
    )(sums)


def solution(mesh):
    return jax.shard_map(
        local,
        mesh=mesh,
        in_specs=(
            P("ctx", "dp"),
            P("ctx", "dp"),
            P("ctx", "dp"),
            P(None, None, "dp"),
            P("dp", None),
            P("ctx", "dp"),
        ),
        out_specs=(P(None, None, "dp"), P("dp", None)),
        check_vma=False,
    )
```

```python
import jax
import jax.numpy as jnp
from jax import lax
from jax.experimental import pallas as pl
from jax.experimental.pallas import tpu as pltpu
from jax.sharding import PartitionSpec as P

MESH = pl.DeviceIdType.MESH
f32, bf16 = jnp.float32, jnp.bfloat16
X, Z = 4, 8
N = X * Z
T = 128
L = 128
TILES = 4
GROUPS = 8
RIM = 16
KS = 7


def halves(x):
    hi = x.astype(bf16)
    lo = (x - hi.astype(f32)).astype(bf16)
    return jnp.concatenate([hi, lo], axis=-1)


def kernel(
    q_hbm, k_hbm, v_hbm, w_hbm, h_hbm, og_hbm, gat,
    q_ref, k_ref, v_ref, w_ref, h_ref, og_ref, toep, halo, rim, qext, kext, vext, wide, lhs, res,
    feats, m2s, g2s, kept, acc, ra, rb,
    loaded, halo_send, halo_recv, rim_send, rim_recv, s1, r1, s2, r2, s3, r3,
):
    me = lax.axis_index("ctx")
    x, z = me // Z, lax.rem(me, Z)
    nxt = {"ctx": lax.rem(me + 1, N)}
    nxt2 = {"ctx": lax.rem(me + 2, N)}
    prv = {"ctx": lax.rem(me + N - 1, N)}
    prv2 = {"ctx": lax.rem(me + N - 2, N)}
    zs = [lax.rem(z + d, Z) for d in (4, 3, 5, 2, 6, 1, 7)]
    xs = [lax.rem(x + d, X) for d in (2, 1, 3)]
    first = me == 0
    final = me == N - 1
    F = TILES // 2

    barrier = pltpu.get_barrier_semaphore()
    partners = [prv, prv2, nxt] + [{"ctx": x * Z + p} for p in zs] + [{"ctx": p * Z + z} for p in xs]
    for p in partners:
        pl.semaphore_signal(barrier, 1, device_id=p, device_id_type=MESH)
    loads = [
        pltpu.make_async_copy(src, dst, loaded.at[n])
        for n, (src, dst) in enumerate(
            ((h_hbm, h_ref), (q_hbm, q_ref), (k_hbm, k_ref), (v_hbm, v_ref), (og_hbm, og_ref), (w_hbm, w_ref))
        )
    ]
    for c in loads:
        c.start()
    pl.semaphore_wait(barrier, len(partners))

    last = pl.ds(T - RIM, RIM)
    half = F * L
    for a, b, p in [
        (q_hbm.at[last], rim.at[:, pl.ds(0, 512)], nxt),
        (k_hbm.at[last], rim.at[:, pl.ds(512, 512)], nxt),
        (v_hbm.at[last], rim.at[:, pl.ds(1024, 512)], nxt),
        (k_hbm.at[last, pl.ds(0, half)], rim.at[:, pl.ds(1536, half)], nxt2),
        (v_hbm.at[last, pl.ds(0, half)], rim.at[:, pl.ds(1792, half)], nxt2),
    ]:
        pltpu.make_async_remote_copy(a, b, rim_send, rim_recv, p, MESH).start()
    order = [t for pair in zip(range(F), range(F, TILES)) for t in pair]
    for t in order:
        pair, p = ((k_hbm, v_hbm), nxt) if t < F else ((q_hbm, og_hbm), prv)
        for n, src in enumerate(pair):
            pltpu.make_async_remote_copy(
                src.at[:, pl.ds(t * L, L)], halo.at[t, n], halo_send.at[t], halo_recv.at[t], p, MESH
            ).start()

    row = lax.broadcasted_iota(jnp.int32, (T, L), 0)
    col = lax.broadcasted_iota(jnp.int32, (T, L), 1)
    flip = jnp.where(lax.rem(row + col, L) == 0, 1.0, 0.0).astype(bf16)
    loads[0].wait()
    taps = h_ref[...].astype(f32)
    flipped = jnp.dot(h_ref[...], flip, preferred_element_type=f32)
    for g in range(TILES * GROUPS):
        for way, src in ((0, flipped), (1, taps)):
            ring = pltpu.roll(
                jnp.broadcast_to(src[g : g + 1], (T, L)), 0, 1, stride=1, stride_axis=0
            )
            near = (col <= row) if way == 0 else (row <= col)
            toep[way, 0, g] = jnp.where(near, ring, 0.0).astype(bf16)
            toep[way, 1, g] = jnp.where(near, 0.0, ring).astype(bf16)

    for c in loads[1:]:
        c.wait()
    for t in range(TILES):
        lanes = slice(t * L, (t + 1) * L)
        qext[t, 8 : 8 + T] = q_ref[:, lanes].astype(f32)
        kext[t, 8 + T :] = k_ref[:, lanes].astype(f32)
        vext[t, 8 + T :] = v_ref[:, lanes].astype(f32)

    def unless(cond, v):
        return jnp.where(cond, 0.0, v.astype(f32))

    def featurize(stream, ext, t, start, rows):
        w = w_ref[stream, :, t * L : (t + 1) * L].astype(f32)
        total = w[0:1] * ext[t, pl.ds(start, rows)]
        for j in range(1, KS):
            total = total + w[j : j + 1] * ext[t, pl.ds(start - j, rows)]
        return total

    def tap_grad(kind, t, ext, parts):
        rows = []
        for j in range(KS):
            total = jnp.zeros((8, L), f32)
            for start, g in parts:
                total = total + jnp.sum((g * ext[t, pl.ds(start - j, T)]).reshape(T // 8, 8, L), axis=0)
            rows.append(jnp.sum(total, axis=0, keepdims=True))
        return jnp.concatenate(rows + [jnp.zeros((1, L), f32)], axis=0)

    lane_group = col // 16
    wide_group = jnp.concatenate([lane_group, lane_group], axis=1)
    mask = [jnp.where(wide_group == g, 1.0, 0.0).astype(bf16) for g in range(GROUPS)]
    inside, across, both = (0,), (1,), (0, 1)
    nt = (((1,), (1,)), ((), ()))
    turn = [0]

    def result():
        turn[0] = (turn[0] + 1) % res.shape[0]
        return res.at[turn[0]]

    def conv(way, lags, t, field):
        out = result()
        filt = [toep[way, n, t * GROUPS : (t + 1) * GROUPS].reshape(GROUPS * T, T) for n in lags]
        filt = jnp.concatenate(filt, axis=1)
        out[...] = jnp.dot(filt, field, preferred_element_type=f32)
        total = out[0:T, :L] + out[0:T, L:]
        for g in range(1, GROUPS):
            total = jnp.where(lane_group == g, out[g * T : (g + 1) * T, :L] + out[g * T : (g + 1) * T, L:], total)
        return total

    def lag_sums(mix, grad, far):
        hi, lo = grad[:, :L], grad[:, L:]
        rhs = jnp.concatenate([jnp.concatenate([hi, hi], 1), jnp.concatenate([lo, lo], 1)], 0)
        for g in range(GROUPS):
            lhs[g * T : (g + 1) * T] = mix * mask[g]
        out = result()
        out[...] = lax.dot_general(lhs[...], rhs, nt, preferred_element_type=f32)
        near = row <= col
        for g in range(GROUPS):
            own = out[g * T : (g + 1) * T, :L] + out[g * T : (g + 1) * T, L:]
            own = jnp.where(near, 0.0, own) if far else jnp.where(near, own, 0.0)
            total = own[0:8]
            for i in range(1, T // 8):
                total = total + pltpu.roll(own[8 * i : 8 * i + 8], L - 8 * i, 1)
            wide[8 * g : 8 * g + 8] = total
        total = wide[pl.ds(0, 8, stride=8)]
        for r in range(1, 8):
            total = total + pltpu.roll(wide[pl.ds(r, 8, stride=8)], L - r, 1)
        return total

    def own_fields(t, start, rows):
        k_own = featurize(1, kext, t, 8 + T + start, rows)
        v_own = featurize(2, vext, t, 8 + T + start, rows)
        og = og_ref[start : start + rows, t * L : (t + 1) * L].astype(f32)
        feats[t, 0, start : start + rows] = k_own
        feats[t, 1, start : start + rows] = v_own
        m2s[t, start : start + rows] = halves(k_own * v_own)
        g2s[t, start : start + rows] = halves(og * featurize(0, qext, t, 8 + start, rows))

    for t in order:
        own_fields(t, RIM, T - RIM)
    pltpu.make_async_copy(rim, rim, rim_recv).wait()
    for t in range(TILES):
        lanes = slice(t * L, (t + 1) * L)
        qext[t, 0:8] = unless(first, rim[8:16, lanes])
        kext[t, T : T + 8] = unless(first, rim[8:16, 512 + t * L : 512 + (t + 1) * L])
        vext[t, T : T + 8] = unless(first, rim[8:16, 1024 + t * L : 1024 + (t + 1) * L])
        if t < F:
            kext[t, 0:8] = unless(me <= 1, rim[8:16, 1536 + t * L : 1536 + (t + 1) * L])
            vext[t, 0:8] = unless(me <= 1, rim[8:16, 1792 + t * L : 1792 + (t + 1) * L])

    for t in order:
        og = og_ref[:, t * L : (t + 1) * L].astype(f32)
        own_fields(t, 0, RIM)
        k_own, v_own = feats[t, 0], feats[t, 1]
        if t < F:
            back = conv(1, inside, t, g2s[t])
            kept[t] = conv(1, across, t, g2s[t])
            acc[t, 1] = tap_grad(1, t, kext, [(8 + T, back * v_own)])
            acc[t, 2] = tap_grad(2, t, vext, [(8 + T, back * k_own)])
        else:
            out = conv(0, inside, t, m2s[t])
            kept[t] = conv(0, across, t, m2s[t])
            acc[t, 0] = tap_grad(0, t, qext, [(8, og * out)])
        acc[t, 3] = lag_sums(m2s[t], g2s[t], False)

    for t in order:
        pltpu.make_async_copy(halo.at[t], halo.at[t], halo_recv.at[t]).wait()
        if t < F:
            kext[t, 8 : 8 + T] = unless(first, halo[t, 0])
            vext[t, 8 : 8 + T] = unless(first, halo[t, 1])
            og = og_ref[:, t * L : (t + 1) * L].astype(f32)
            k_prev = featurize(1, kext, t, 8, T)
            v_prev = featurize(2, vext, t, 8, T)
            mp2 = halves(k_prev * v_prev)
            out = conv(0, both, t, jnp.concatenate([m2s[t], mp2], axis=0))
            back = kept[t]
            acc[t, 0] = tap_grad(0, t, qext, [(8, og * out)])
            acc[t, 1] += tap_grad(1, t, kext, [(8, back * v_prev)])
            acc[t, 2] += tap_grad(2, t, vext, [(8, back * k_prev)])
            acc[t, 3] += lag_sums(mp2, g2s[t], True)
        else:
            qext[t, 8 + T :] = unless(final, halo[t, 0])
            og_next = unless(final, halo[t, 1])
            gn2 = halves(og_next * featurize(0, qext, t, 8 + T, T))
            back = conv(1, both, t, jnp.concatenate([g2s[t], gn2], axis=0))
            acc[t, 0] += tap_grad(0, t, qext, [(8 + T, og_next * kept[t])])
            acc[t, 1] = tap_grad(1, t, kext, [(8 + T, back * feats[t, 1])])
            acc[t, 2] = tap_grad(2, t, vext, [(8 + T, back * feats[t, 0])])
            acc[t, 3] += lag_sums(m2s[t], gn2, True)

        @pl.when(x != t)
        def _():
            pltpu.make_async_remote_copy(acc.at[t], ra.at[x], s1, r1, {"ctx": t * Z + z}, MESH).start()

    ra[x] = acc[x]
    three = ra.at[pl.ds(0, X - 1)]
    seven = rb.at[pl.ds(0, Z - 1)]
    pltpu.make_async_copy(three, three, r1).wait()
    total = ra[0]
    for i in range(1, X):
        total = total + ra[i]
    rb[z] = total
    for p in zs:
        pltpu.make_async_remote_copy(rb.at[z], rb.at[z], s2, r2, {"ctx": x * Z + p}, MESH).start()
    pltpu.make_async_copy(seven, seven, r2).wait()
    total = rb[0]
    for i in range(1, Z):
        total = total + rb[i]
    gat[x] = total
    for p in xs:
        pltpu.make_async_remote_copy(gat.at[x], gat.at[x], s3, r3, {"ctx": p * Z + z}, MESH).start()
    gathered = gat.at[pl.ds(0, X - 1)]
    pltpu.make_async_copy(gathered, gathered, r3).wait()
    for t in order:
        pltpu.make_async_copy(halo.at[t], halo.at[t], halo_send.at[t]).wait()
    pltpu.make_async_copy(rim, rim, rim_send).wait()
    pltpu.make_async_copy(three, three, s1).wait()
    pltpu.make_async_copy(seven, seven, s2).wait()
    pltpu.make_async_copy(gathered, gathered, s3).wait()


def spread(gat, s_ref, m_ref):
    for t in range(TILES):
        for kind in range(3):
            s_ref[kind, :, t * L : (t + 1) * L] = gat[t, kind, :KS]
        m_ref[t * GROUPS : (t + 1) * GROUPS] = gat[t, 3]


def local(q, k, v, w, h, og):
    V = pltpu.VMEM
    dma = pltpu.SemaphoreType.DMA
    hbm, vmem = pl.BlockSpec(memory_space=pltpu.HBM), pl.BlockSpec(memory_space=V)
    sums = pl.pallas_call(
        kernel,
        out_shape=pltpu.VMEM((TILES, 4, 8, L), f32),
        in_specs=[hbm] * 6,
        out_specs=vmem,
        scratch_shapes=[
            V((T, 512), bf16), V((T, 512), bf16), V((T, 512), bf16), V((3, KS, 512), bf16), V((32, T), bf16), V((T, 512), bf16),
            V((2, 2, TILES * GROUPS, T, T), bf16),
            V((TILES, 2, T, L), bf16),
            V((RIM, 2048), bf16),
            V((TILES, 8 + 2 * T, L), f32),
            V((TILES, 8 + 2 * T, L), f32),
            V((TILES, 8 + 2 * T, L), f32),
            V((8 * GROUPS, L), f32),
            V((GROUPS * T, 2 * L), bf16),
            V((4, GROUPS * T, 2 * L), f32),
            V((TILES, 2, T, L), f32),
            V((TILES, T, 2 * L), bf16),
            V((TILES, T, 2 * L), bf16),
            V((TILES, T, L), f32),
            V((TILES, 4, 8, L), f32),
            V((X, 4, 8, L), f32),
            V((Z, 4, 8, L), f32),
            dma((6,)), dma((TILES,)), dma((TILES,)),
            dma, dma, dma, dma, dma, dma, dma, dma,
        ],
        compiler_params=pltpu.CompilerParams(
            collective_id=0, has_side_effects=True, vmem_limit_bytes=56 << 20
        ),
        name="block",
    )(q, k, v, w, h, og)
    return pl.pallas_call(
        spread,
        out_shape=(jax.ShapeDtypeStruct((3, KS, 512), f32), jax.ShapeDtypeStruct((32, 128), f32)),
        in_specs=[vmem],
        out_specs=[vmem, vmem],
        compiler_params=pltpu.CompilerParams(vmem_limit_bytes=1 << 20),
        name="spread",
    )(sums)


def solution(mesh):
    return jax.shard_map(
        local,
        mesh=mesh,
        in_specs=(
            P("ctx", "dp"),
            P("ctx", "dp"),
            P("ctx", "dp"),
            P(None, None, "dp"),
            P("dp", None),
            P("ctx", "dp"),
        ),
        out_specs=(P(None, None, "dp"), P("dp", None)),
        check_vma=False,
    )
```
